32 devices in a mesh: pipe: 4 (over z), dp: 2 (over y), tensor: 4 (over x, core).
Axes of the slice: x: 2, y: 2, z: 4, core: 2. Of those that a mesh axis runs over, the one named last changes fastest.
Arguments:
- hidden_in: bfloat16 [8, 512, 8192], P(('pipe', 'dp'), None, 'tensor'), may hold values from -8 to 8
- norm_gain: bfloat16 [8192], P('tensor'), may hold values from 0.099609375 to 1.8984375
- queries: bfloat16 [8, 512, 8192], P(('pipe', 'dp'), None, 'tensor'), may hold values from -12 to 12
- key_weight: bfloat16 [8192, 1024], P('pipe', 'tensor'), may hold values from -1 to 1
- value_weight: bfloat16 [8192, 1024], P('pipe', 'tensor'), may hold values from -0.0625 to 0.0625
- out_grad: bfloat16 [8, 512, 8192], P(('pipe', 'dp'), None, 'tensor'), may hold values from -6 to 6
Outputs:
- attended: bfloat16 [8, 512, 8192], P(('pipe', 'dp'), None, 'tensor')
- key_grad: float32 [8192, 1024], P('pipe', 'tensor')
- value_grad: float32 [8192, 1024], P('pipe', 'tensor')
The draws below stay inside these ranges and needn't reach their ends.
All inputs are finite; a program needn't handle non-finite values.
Results may differ from the reference program's by a relative error of at most 0.013.
The reference program's roundings to bfloat16 on the way (of `normed`, `keys`, `probs_low`, `dscores`, `dvalues` and `dkeys`) count: a program that leaves them out, or rounds other values in their place, can miss the bound.
Values may be sent and summed in bfloat16 or wider, within the bound.
A program may use at most 128 MiB of HBM per device.

```python
import math
import jax
import jax.numpy as jnp
from jax import lax

D = 8192
QH = 64
KVH = 8
HD = 128
ROWS = 512
GROUP = 8
MB = 8


def draw_hidden_in(key, part):
    key = jax.random.fold_in(key, 1)
    sample = jax.random.truncated_normal(key, -6.0, 6.0, (MB, ROWS, D), jnp.float32)
    return sample.astype(jnp.bfloat16)


def draw_key_weight(key, part):
    key = jax.random.fold_in(key, 2)
    sample = jax.random.truncated_normal(key, -6.0, 6.0, (D, KVH * HD), jnp.float32) / math.sqrt(D)
    return sample.astype(jnp.bfloat16)


def draw_queries(key, part):
    key = jax.random.fold_in(key, 3)
    sample = jax.random.truncated_normal(key, -6.0, 6.0, (MB, ROWS, QH * HD), jnp.float32)
    return sample.astype(jnp.bfloat16)


def levels(own_key, extent, split, least, high):
    def one(dim, blocks):
        draws = jax.random.uniform(jax.random.fold_in(jax.random.fold_in(own_key, 6), dim), (blocks,), jnp.float32, least / len(split), high / len(split))
        return jnp.repeat(jnp.exp(draws), extent[dim] // blocks).reshape((-1,) + (1,) * (len(extent) - dim - 1))

    level = one(*split[0])
    for cut in split[1:]:
        level = level * one(*cut)
    return level


def centred(own_key, extent, spread, limit, split=(), kind=jnp.bfloat16):
    drawn = jax.random.normal(own_key, extent, jnp.float32) * spread
    if len(split) > 0:
        drawn = levels(own_key, extent, split, -0.22, 0.18) * drawn
    return jnp.clip(drawn, min=-limit, max=limit).astype(kind)


def setup_inputs(seed: int = 0) -> dict:
    arg_keys = jax.random.split(jax.random.key(seed), 7)
    return {
        "hidden_in": draw_hidden_in(jax.random.fold_in(arg_keys[6], 71), 0),
        "norm_gain": jnp.clip(1.0 + 0.18 * jax.random.normal(arg_keys[1], (D,), jnp.float32), 0.099609375, 1.8984375).astype(jnp.bfloat16),
        "queries": draw_queries(jax.random.fold_in(arg_keys[6], 71), 0),
        "key_weight": draw_key_weight(jax.random.fold_in(arg_keys[6], 71), 0),
        "value_weight": centred(arg_keys[4], (D, KVH * HD), D ** -0.5, 0.0625, ((0, 4), (1, 4))),
        "out_grad": centred(arg_keys[5], (MB, ROWS, QH * HD), 1.0, 6.0, ((0, 8), (2, 4))),
    }


def one_batch(hidden, gain, query, cotangent, key_weight, value_weight):
    scale = 1.0 / HD ** 0.5
    wide = hidden.astype(jnp.float32)
    power = lax.optimization_barrier(jnp.mean(wide * wide, axis=-1, keepdims=True))
    normed = (wide * lax.rsqrt(power + 1e-05) * gain.astype(jnp.float32)).astype(jnp.bfloat16)
    keys = jnp.dot(normed, key_weight, preferred_element_type=jnp.float32).astype(jnp.bfloat16)
    values = jnp.dot(normed, value_weight, preferred_element_type=jnp.float32).astype(jnp.bfloat16)
    query_heads = query.reshape(ROWS, KVH, GROUP, HD).astype(jnp.float32)
    key_heads = keys.reshape(ROWS, KVH, HD).astype(jnp.float32)
    value_heads = values.reshape(ROWS, KVH, HD).astype(jnp.float32)
    scores = jnp.einsum('qhgd,khd->hgqk', query_heads, key_heads) * scale
    position = jnp.arange(ROWS, dtype=jnp.int32)
    visible = position[:, None] >= position[None, :]
    scores = jnp.where(visible, scores, -1e+30)
    probs = jax.nn.softmax(scores, axis=-1)
    probs_low = probs.astype(jnp.bfloat16).astype(jnp.float32)
    attended = jnp.einsum('hgqk,khd->qhgd', probs_low, value_heads).reshape(ROWS, QH * HD).astype(jnp.bfloat16)
    grad_heads = cotangent.reshape(ROWS, KVH, GROUP, HD).astype(jnp.float32)
    dprobs = jnp.einsum('qhgd,khd->hgqk', grad_heads, value_heads)
    inner = lax.optimization_barrier(jnp.sum(dprobs * probs, axis=-1, keepdims=True))
    dscores = (probs * (dprobs - inner) * scale).astype(jnp.bfloat16).astype(jnp.float32)
    dvalues = jnp.einsum('hgqk,qhgd->khd', probs_low, grad_heads).reshape(ROWS, KVH * HD).astype(jnp.bfloat16)
    dkeys = jnp.einsum('hgqk,qhgd->khd', dscores, query_heads).reshape(ROWS, KVH * HD).astype(jnp.bfloat16)
    key_term = jnp.dot(normed.T, dkeys, preferred_element_type=jnp.float32)
    value_term = jnp.dot(normed.T, dvalues, preferred_element_type=jnp.float32)
    return (attended, key_term, value_term)

def reference(hidden_in, norm_gain, queries, key_weight, value_weight, out_grad):

    def step(carry, items):
        hidden, query, cotangent = items
        attended, key_term, value_term = one_batch(hidden, norm_gain, query, cotangent, key_weight, value_weight)
        return ((carry[0] + key_term, carry[1] + value_term), attended)
    start = (jnp.zeros((D, KVH * HD), jnp.float32), jnp.zeros((D, KVH * HD), jnp.float32))
    totals, attended = lax.scan(step, start, (hidden_in, queries, out_grad))
    return (attended, totals[0], totals[1])
```

```python
import functools
import jax
import jax.numpy as jnp
from jax import lax
from jax.experimental import pallas as pl
from jax.experimental.pallas import tpu as pltpu
from jax.sharding import PartitionSpec as P

HD = 128
GROUP = 8
MESH = pl.DeviceIdType.MESH


def gather_kernel(
    n, hc, wc, h_in, g_in, k_in, v_in, h_out, g_out, k_out, v_out,
    loc_sem, hx_s, hx_r, hs_s, hs_r, hf_s, hf_r, g_s, g_r, zu_s, zd_s, z_r, y_s, y_r,
):
    p = lax.axis_index("pipe")
    d = lax.axis_index("dp")
    t = lax.axis_index("tensor")
    a, c = t // 2, t % 2
    across, sibling = (1 - a) * 2 + c, a * 2 + (1 - c)
    far = (1 - a) * 2 + (1 - c)
    rows, width = h_in.shape
    depth = k_in.shape[0]
    half = depth // 2
    piece = half // wc
    hrows = rows // hc

    barrier = pltpu.get_barrier_semaphore()
    for peer in (across, sibling, far):
        pl.semaphore_signal(barrier, inc=1, device_id=(p, d, peer), device_id_type=MESH)
    pl.semaphore_signal(barrier, inc=1, device_id=(p, 1 - d, t), device_id_type=MESH)

    for peer in (lax.rem(p + 1, n), lax.rem(p + n - 1, n)):
        pl.semaphore_signal(barrier, inc=1, device_id=(peer, d, t), device_id_type=MESH)
    pl.semaphore_wait(barrier, 6)

    def remote(src, dst, ssem, rsem, dev):
        return pltpu.make_async_remote_copy(
            src_ref=src, dst_ref=dst, send_sem=ssem, recv_sem=rsem, device_id=dev, device_id_type=MESH
        )

    def cols(i):
        return pl.ds(pl.multiple_of(i * width, width), width)

    def hslice(ref, i, k):
        return ref.at[pl.ds(k * hrows, hrows), cols(i)]

    def hown(k):
        return h_in.at[pl.ds(k * hrows, hrows)]

    def x_copy(k, owner):
        return remote(hown(k), hslice(h_out, owner, k), hx_s.at[k], hx_r.at[k], (p, d, across))

    def sib_copy(k, owner):
        return remote(hown(k), hslice(h_out, owner, k), hs_s.at[k], hs_r.at[k], (p, d, sibling))

    def fwd_copy(k, owner):
        return remote(
            hslice(h_out, owner, k), hslice(h_out, owner, k), hf_s.at[k], hf_r.at[k], (p, d, sibling)
        )

    def wpart(ref, b, k, hd):
        return ref.at[b, pl.ds(hd * half + (k % wc) * piece, piece)]

    def wout(k):
        return k_out if k < wc else v_out

    def wsrc(k):
        return (k_in if k < wc else v_in).at[pl.ds(d * half + (k % wc) * piece, piece)]

    def z_copy(src, b, k, up):
        dev = (p + 1, d, t) if up else (p - 1, d, t)
        sem = zu_s if up else zd_s
        return remote(src, wpart(wout(k), b, k, d), sem.at[b, k], z_r.at[b, k], dev)

    def y_copy(b, k, hd):
        part = wpart(wout(k), b, k, hd)
        return remote(part, part, y_s.at[b, k], y_r.at[b, k], (p, 1 - d, t))

    for k in range(2 * wc):

        @pl.when(p < n - 1)
        def _(k=k):
            z_copy(wsrc(k), p, k, True).start()

        @pl.when(p > 0)
        def _(k=k):
            z_copy(wsrc(k), p, k, False).start()

    gains = [
        remote(g_in, g_out.at[t], g_s.at[i], g_r.at[i], (p, d, peer))
        for i, peer in enumerate((across, sibling, far))
    ]
    for copy in gains:
        copy.start()
    for k in range(hc):
        x_copy(k, t).start()
    for k in range(hc):
        sib_copy(k, t).start()
    local = [
        pltpu.make_async_copy(h_in, h_out.at[:, cols(t)], loc_sem.at[0]),
        pltpu.make_async_copy(g_in, g_out.at[t], loc_sem.at[1]),
        pltpu.make_async_copy(k_in, k_out.at[p], loc_sem.at[2]),
        pltpu.make_async_copy(v_in, v_out.at[p], loc_sem.at[3]),
    ]
    for copy in local:
        copy.start()

    def hidden_step(k):
        x_copy(k, across).wait_recv()
        fwd_copy(k, across).start()

    done = 0
    for s in range(1, n):
        for k in range(2 * wc):

            @pl.when(p - s >= 0)
            def _(s=s, k=k):
                b = p - s
                z_copy(wsrc(k), b, k, True).wait_recv()

                @pl.when(p < n - 1)
                def _():
                    z_copy(wpart(wout(k), b, k, d), b, k, True).start()

                y_copy(b, k, d).start()

            @pl.when(p + s < n)
            def _(s=s, k=k):
                b = p + s
                z_copy(wsrc(k), b, k, False).wait_recv()

                @pl.when(p > 0)
                def _():
                    z_copy(wpart(wout(k), b, k, d), b, k, False).start()

                y_copy(b, k, d).start()

        goal = hc if s == n - 1 else min(hc, (hc * s) // (n - 1))
        while done < goal:
            hidden_step(done)
            done += 1

    for s in range(1, n):
        for k in range(2 * wc):
            for up in (True, False):
                b = p - s if up else p + s

                @pl.when((b >= 0) & (b < n))
                def _(b=b, k=k):
                    y_copy(b, k, 1 - d).wait_recv()
                    y_copy(b, k, d).wait_send()

    for s in range(n):
        for k in range(2 * wc):

            @pl.when((p - s >= 0) & (p < n - 1))
            def _(s=s, k=k):
                z_copy(wsrc(k), p - s, k, True).wait_send()

            @pl.when((p + s < n) & (p > 0))
            def _(s=s, k=k):
                z_copy(wsrc(k), p + s, k, False).wait_send()

    for k in range(hc):
        sib_copy(k, sibling).wait_recv()
        fwd_copy(k, far).wait_recv()
        x_copy(k, t).wait_send()
        sib_copy(k, t).wait_send()
        fwd_copy(k, across).wait_send()
    for i, peer in enumerate((across, sibling, far)):
        remote(g_in, g_out.at[peer], g_s.at[i], g_r.at[i], (p, d, peer)).wait_recv()
    for copy in gains:
        copy.wait_send()
    for copy in local:
        copy.wait()


def gather_all(n, hidden, gain, key_weight, value_weight):
    rows, width = hidden.shape
    depth, kv = key_weight.shape
    gain = gain.reshape(-1, 128)
    hc = 4
    wc = 2 if n <= 8 else 1
    dma = pltpu.SemaphoreType.DMA
    any_spec = pl.BlockSpec(memory_space=pl.ANY)
    return pl.pallas_call(
        functools.partial(gather_kernel, n, hc, wc),
        out_shape=[
            jax.ShapeDtypeStruct((rows, 4 * width), hidden.dtype),
            jax.ShapeDtypeStruct((4,) + gain.shape, gain.dtype),
            jax.ShapeDtypeStruct((n, depth, kv), key_weight.dtype),
            jax.ShapeDtypeStruct((n, depth, kv), value_weight.dtype),
        ],
        in_specs=[any_spec] * 4,
        out_specs=[any_spec] * 4,
        scratch_shapes=[
            dma((4,)),
            dma((hc,)), dma((hc,)), dma((hc,)), dma((hc,)), dma((hc,)), dma((hc,)),
            dma((3,)), dma((3,)),
            dma((n, 2 * wc)), dma((n, 2 * wc)), dma((n, 2 * wc)), dma((n, 2 * wc)), dma((n, 2 * wc)),
        ],
        compiler_params=pltpu.CompilerParams(collective_id=0, has_side_effects=True),
        name="gather_inputs",
    )(hidden, gain, key_weight, value_weight)


def shards(n, hidden_in, norm_gain, queries, key_weight, value_weight, out_grad):
    scale = 1.0 / HD**0.5
    pipe = lax.axis_index("pipe")
    tensor = lax.axis_index("tensor")
    depth, kv_width = key_weight.shape
    whole, gains, all_key, all_value = gather_all(n, hidden_in[0], norm_gain, key_weight, value_weight)
    wide = whole.astype(jnp.float32)
    power = jnp.mean(wide * wide, axis=-1, keepdims=True)
    normed = (wide * lax.rsqrt(power + 1e-05) * gains.reshape(-1).astype(jnp.float32)).astype(jnp.bfloat16)
    tokens = normed.shape[0]
    local_heads = kv_width // HD

    quarter = tokens // 4
    mine = lax.dynamic_slice_in_dim(normed, tensor * quarter, quarter, 0)
    parts = []
    for s in range(n):
        dest = lax.rem(pipe + s, n)
        block = lax.dynamic_slice_in_dim(mine, dest * depth, depth, 1)
        if s:
            block = lax.ppermute(block, "pipe", [(i, (i + s) % n) for i in range(n)])
        parts.append(block)
    columns = lax.all_gather(jnp.stack(parts), "tensor", axis=0)

    keys = jnp.dot(normed, all_key.reshape(-1, kv_width), preferred_element_type=jnp.float32)
    values = jnp.dot(normed, all_value.reshape(-1, kv_width), preferred_element_type=jnp.float32)
    keys = keys.astype(jnp.bfloat16).reshape(tokens, local_heads, HD)
    values = values.astype(jnp.bfloat16).reshape(tokens, local_heads, HD)
    query_heads = queries[0].reshape(tokens, local_heads, GROUP, HD)
    grad_heads = out_grad[0].reshape(tokens, local_heads, GROUP, HD)
    scores = (
        jnp.einsum("qhgd,khd->hgqk", query_heads, keys, preferred_element_type=jnp.float32) * scale
    )
    position = jnp.arange(tokens, dtype=jnp.int32)
    visible = position[:, None] >= position[None, :]
    scores = jnp.where(visible, scores, -1e30)
    probs = jax.nn.softmax(scores, axis=-1)
    probs_low = probs.astype(jnp.bfloat16)
    attended = jnp.einsum("hgqk,khd->qhgd", probs_low, values, preferred_element_type=jnp.float32)
    attended = attended.reshape(1, tokens, local_heads * GROUP * HD).astype(jnp.bfloat16)
    dprobs = jnp.einsum("qhgd,khd->hgqk", grad_heads, values, preferred_element_type=jnp.float32)
    inner = jnp.sum(dprobs * probs, axis=-1, keepdims=True)
    dscores = (probs * (dprobs - inner) * scale).astype(jnp.bfloat16)
    dvalues = jnp.einsum(
        "hgqk,qhgd->khd", probs_low, grad_heads, preferred_element_type=jnp.float32
    )
    dkeys = jnp.einsum("hgqk,qhgd->khd", dscores, query_heads, preferred_element_type=jnp.float32)
    combined = jnp.concatenate(
        [
            dkeys.reshape(tokens, kv_width).astype(jnp.bfloat16),
            dvalues.reshape(tokens, kv_width).astype(jnp.bfloat16),
        ],
        axis=1,
    )
    every = lax.all_gather(combined, "pipe", axis=0)
    partial_sum = None
    for s in range(n):
        source = lax.rem(pipe + n - s, n)
        theirs = lax.dynamic_index_in_dim(every, source, 0, keepdims=False)
        term = lax.dot_general(
            columns[:, s].reshape(tokens, depth), theirs, (((0,), (0,)), ((), ())),
            preferred_element_type=jnp.float32,
        )
        partial_sum = term if partial_sum is None else partial_sum + term
    total = partial_sum + lax.ppermute(partial_sum, "dp", [(0, 1), (1, 0)])
    return (attended, total[:, :kv_width], total[:, kv_width:])


def solution(mesh):
    placed = (
        P(("pipe", "dp"), None, "tensor"),
        P("tensor"),
        P(("pipe", "dp"), None, "tensor"),
        P("pipe", "tensor"),
        P("pipe", "tensor"),
        P(("pipe", "dp"), None, "tensor"),
    )
    return jax.shard_map(
        functools.partial(shards, mesh.shape["pipe"]),
        mesh=mesh,
        in_specs=placed,
        out_specs=(P(("pipe", "dp"), None, "tensor"), P("pipe", "tensor"), P("pipe", "tensor")),
        check_vma=False,
    )
```

```python
import functools
import jax
import jax.numpy as jnp
from jax import lax
from jax.experimental import pallas as pl
from jax.experimental.pallas import tpu as pltpu
from jax.sharding import PartitionSpec as P

HD = 128
GROUP = 8
MESH = pl.DeviceIdType.MESH


def gather_kernel(
    n, hc, wc, h_in, g_in, k_in, v_in, h_out, g_out, k_out, v_out,
    loc_sem, hx_s, hx_r, hs_s, hs_r, hf_s, hf_r, g_s, g_r, zu_s, zd_s, z_r, y_s, y_r,
):
    p = lax.axis_index("pipe")
    d = lax.axis_index("dp")
    t = lax.axis_index("tensor")
    a, c = t // 2, t % 2
    across, sibling = (1 - a) * 2 + c, a * 2 + (1 - c)
    far = (1 - a) * 2 + (1 - c)
    rows, width = h_in.shape
    depth = k_in.shape[0]
    half = depth // 2
    piece = half // wc
    hrows = rows // hc

    barrier = pltpu.get_barrier_semaphore()
    for peer in (across, sibling, far):
        pl.semaphore_signal(barrier, inc=1, device_id=(p, d, peer), device_id_type=MESH)
    pl.semaphore_signal(barrier, inc=1, device_id=(p, 1 - d, t), device_id_type=MESH)

    for peer in (lax.rem(p + 1, n), lax.rem(p + n - 1, n)):
        pl.semaphore_signal(barrier, inc=1, device_id=(peer, d, t), device_id_type=MESH)
    pl.semaphore_wait(barrier, 6)

    def remote(src, dst, ssem, rsem, dev):
        return pltpu.make_async_remote_copy(
            src_ref=src, dst_ref=dst, send_sem=ssem, recv_sem=rsem, device_id=dev, device_id_type=MESH
        )

    def cols(i):
        return pl.ds(pl.multiple_of(i * width, width), width)

    def hslice(ref, i, k):
        return ref.at[pl.ds(k * hrows, hrows), cols(i)]

    def hown(k):
        return h_in.at[pl.ds(k * hrows, hrows)]

    def x_copy(k, owner):
        return remote(hown(k), hslice(h_out, owner, k), hx_s.at[k], hx_r.at[k], (p, d, across))

    def sib_copy(k, owner):
        return remote(hown(k), hslice(h_out, owner, k), hs_s.at[k], hs_r.at[k], (p, d, sibling))

    def fwd_copy(k, owner):
        return remote(
            hslice(h_out, owner, k), hslice(h_out, owner, k), hf_s.at[k], hf_r.at[k], (p, d, sibling)
        )

    def wpart(ref, b, k, hd):
        return ref.at[b, pl.ds(hd * half + (k % wc) * piece, piece)]

    def wout(k):
        return k_out if k < wc else v_out

    def wsrc(k):
        return (k_in if k < wc else v_in).at[pl.ds(d * half + (k % wc) * piece, piece)]

    def z_copy(src, b, k, up):
        dev = (p + 1, d, t) if up else (p - 1, d, t)
        sem = zu_s if up else zd_s
        return remote(src, wpart(wout(k), b, k, d), sem.at[b, k], z_r.at[b, k], dev)

    def y_copy(b, k, hd):
        part = wpart(wout(k), b, k, hd)
        return remote(part, part, y_s.at[b, k], y_r.at[b, k], (p, 1 - d, t))

    for k in range(2 * wc):

        @pl.when(p < n - 1)
        def _(k=k):
            z_copy(wsrc(k), p, k, True).start()

        @pl.when(p > 0)
        def _(k=k):
            z_copy(wsrc(k), p, k, False).start()

    gains = [
        remote(g_in, g_out.at[t], g_s.at[i], g_r.at[i], (p, d, peer))
        for i, peer in enumerate((across, sibling, far))
    ]
    for copy in gains:
        copy.start()
    for k in range(hc):
        x_copy(k, t).start()
    for k in range(hc):
        sib_copy(k, t).start()
    local = [
        pltpu.make_async_copy(h_in, h_out.at[:, cols(t)], loc_sem.at[0]),
        pltpu.make_async_copy(g_in, g_out.at[t], loc_sem.at[1]),
        pltpu.make_async_copy(k_in, k_out.at[p], loc_sem.at[2]),
        pltpu.make_async_copy(v_in, v_out.at[p], loc_sem.at[3]),
    ]
    for copy in local:
        copy.start()

    def hidden_step(k):
        x_copy(k, across).wait_recv()
        fwd_copy(k, across).start()

    done = 0
    for s in range(1, n):
        for k in range(2 * wc):

            @pl.when(p - s >= 0)
            def _(s=s, k=k):
                b = p - s
                z_copy(wsrc(k), b, k, True).wait_recv()

                @pl.when(p < n - 1)
                def _():
                    z_copy(wpart(wout(k), b, k, d), b, k, True).start()

                y_copy(b, k, d).start()

            @pl.when(p + s < n)
            def _(s=s, k=k):
                b = p + s
                z_copy(wsrc(k), b, k, False).wait_recv()

                @pl.when(p > 0)
                def _():
                    z_copy(wpart(wout(k), b, k, d), b, k, False).start()

                y_copy(b, k, d).start()

        goal = hc if s == n - 1 else min(hc, (hc * s) // (n - 1))
        while done < goal:
            hidden_step(done)
            done += 1

    for s in range(1, n):
        for k in range(2 * wc):
            for up in (True, False):
                b = p - s if up else p + s

                @pl.when((b >= 0) & (b < n))
                def _(b=b, k=k):
                    y_copy(b, k, 1 - d).wait_recv()
                    y_copy(b, k, d).wait_send()

    for s in range(n):
        for k in range(2 * wc):

            @pl.when((p - s >= 0) & (p < n - 1))
            def _(s=s, k=k):
                z_copy(wsrc(k), p - s, k, True).wait_send()

            @pl.when((p + s < n) & (p > 0))
            def _(s=s, k=k):
                z_copy(wsrc(k), p + s, k, False).wait_send()

    for k in range(hc):
        sib_copy(k, sibling).wait_recv()
        fwd_copy(k, far).wait_recv()
        x_copy(k, t).wait_send()
        sib_copy(k, t).wait_send()
        fwd_copy(k, across).wait_send()
    for i, peer in enumerate((across, sibling, far)):
        remote(g_in, g_out.at[peer], g_s.at[i], g_r.at[i], (p, d, peer)).wait_recv()
    for copy in gains:
        copy.wait_send()
    for copy in local:
        copy.wait()


def gather_all(n, hidden, gain, key_weight, value_weight):
    rows, width = hidden.shape
    depth, kv = key_weight.shape
    gain = gain.reshape(-1, 128)
    hc = 4
    wc = 2 if n <= 8 else 1
    dma = pltpu.SemaphoreType.DMA
    any_spec = pl.BlockSpec(memory_space=pl.ANY)
    return pl.pallas_call(
        functools.partial(gather_kernel, n, hc, wc),
        out_shape=[
            jax.ShapeDtypeStruct((rows, 4 * width), hidden.dtype),
            jax.ShapeDtypeStruct((4,) + gain.shape, gain.dtype),
            jax.ShapeDtypeStruct((n, depth, kv), key_weight.dtype),
            jax.ShapeDtypeStruct((n, depth, kv), value_weight.dtype),
        ],
        in_specs=[any_spec] * 4,
        out_specs=[any_spec] * 4,
        scratch_shapes=[
            dma((4,)),
            dma((hc,)), dma((hc,)), dma((hc,)), dma((hc,)), dma((hc,)), dma((hc,)),
            dma((3,)), dma((3,)),
            dma((n, 2 * wc)), dma((n, 2 * wc)), dma((n, 2 * wc)), dma((n, 2 * wc)), dma((n, 2 * wc)),
        ],
        compiler_params=pltpu.CompilerParams(collective_id=0, has_side_effects=True),
        name="gather_inputs",
    )(hidden, gain, key_weight, value_weight)


def attention_kernel(
    n, normed, q_ref, g_ref, k_ref, v_ref, att_ref, x_out, e_out, comb, acc_k, acc_v,
    loc_sem, z_s, z_r, ac_s, ac_r, sb_s, sb_r, fw_s, fw_r, e_s, e_r,
):
    p = lax.axis_index("pipe")
    d = lax.axis_index("dp")
    t = lax.axis_index("tensor")
    a, c = t // 2, t % 2
    across, sibling = (1 - a) * 2 + c, a * 2 + (1 - c)
    far = (1 - a) * 2 + (1 - c)
    tokens = q_ref.shape[0]
    depth = x_out.shape[2]
    quarter = tokens // 4
    scale = 1.0 / HD**0.5
    local_heads = k_ref.shape[1] // HD
    group = q_ref.shape[1] // HD // local_heads

    barrier = pltpu.get_barrier_semaphore()
    for s in range(1, n):
        pl.semaphore_signal(barrier, inc=1, device_id=(lax.rem(p + s, n), d, t), device_id_type=MESH)
    for peer in (across, sibling):
        pl.semaphore_signal(barrier, inc=1, device_id=(p, d, peer), device_id_type=MESH)
    pl.semaphore_wait(barrier, n + 1)

    def remote(src, dst, ssem, rsem, dev):
        return pltpu.make_async_remote_copy(
            src_ref=src, dst_ref=dst, send_sem=ssem, recv_sem=rsem, device_id=dev, device_id_type=MESH
        )

    def rows(i):
        return pl.ds(pl.multiple_of(i * quarter, quarter), quarter)

    def cols(i):
        return pl.ds(pl.multiple_of(i * depth, depth), depth)

    def z_copy(s):
        dest = lax.rem(p + s, n)
        return remote(
            normed.at[rows(t), cols(dest)], x_out.at[s, rows(t)], z_s.at[s], z_r.at[s], (dest, d, t)
        )

    def share(s, part, ssem, rsem, peer):
        ref = x_out.at[s, rows(part)]
        return remote(ref, ref, ssem.at[s], rsem.at[s], (p, d, peer))

    def e_copy(s, j):
        dest = lax.rem(p + s, n)
        width = pl.ds(j * HD, HD)
        return remote(
            comb.at[:, :, width], e_out.at[:, s, :, width], e_s.at[s, j], e_r.at[s, j], (dest, d, t)
        )

    def e_local(j):
        width = pl.ds(j * HD, HD)
        return pltpu.make_async_copy(comb.at[:, :, width], e_out.at[:, 0, :, width], loc_sem.at[1 + j])

    def pass_on(s):
        z_copy(s).wait_recv()
        share(s, t, ac_s, ac_r, across).start()
        share(s, t, sb_s, sb_r, sibling).start()

    def pass_over(s):
        share(s, across, ac_s, ac_r, across).wait_recv()
        share(s, across, fw_s, fw_r, sibling).start()

    for s in range(1, n):
        z_copy(s).start()
    own = pltpu.make_async_copy(normed.at[:, cols(p)], x_out.at[0], loc_sem.at[0])
    own.start()

    blocks = 2
    size = tokens // blocks
    nt = (((1,), (1,)), ((), ()))
    tn = (((0,), (0,)), ((), ()))
    f32 = jnp.float32
    for j in range(local_heads):
        acc_k[...] = jnp.zeros_like(acc_k)
        acc_v[...] = jnp.zeros_like(acc_v)

        def head(i, carry, j=j):
            at = pl.ds(pl.multiple_of((j * group + i) * HD, HD), HD)
            for b in range(blocks):
                low, high = b * size, (b + 1) * size
                q = q_ref[low:high, at]
                g = g_ref[low:high, at]
                k = k_ref[:high, j * HD : (j + 1) * HD]
                v = v_ref[:high, j * HD : (j + 1) * HD]
                scores = lax.dot_general(q, k, nt, preferred_element_type=f32) * scale
                qpos = low + lax.broadcasted_iota(jnp.int32, scores.shape, 0)
                kpos = lax.broadcasted_iota(jnp.int32, scores.shape, 1)
                scores = jnp.where(qpos >= kpos, scores, -1e30)
                top = jnp.max(scores, axis=-1, keepdims=True)
                e = jnp.exp(scores - top)
                probs = e * (1.0 / jnp.sum(e, axis=-1, keepdims=True))
                low_probs = probs.astype(jnp.bfloat16)
                att = jnp.dot(low_probs, v, preferred_element_type=f32)
                att_ref[low:high, at] = att.astype(jnp.bfloat16)
                dprobs = lax.dot_general(g, v, nt, preferred_element_type=f32)
                inner = jnp.sum(dprobs * probs, axis=-1, keepdims=True)
                dscores = (probs * (dprobs - inner) * scale).astype(jnp.bfloat16)
                acc_v[:high] += lax.dot_general(low_probs, g, tn, preferred_element_type=f32)
                acc_k[:high] += lax.dot_general(dscores, q, tn, preferred_element_type=f32)
            return carry

        lax.fori_loop(0, group, head, 0)
        comb[0, :, j * HD : (j + 1) * HD] = acc_k[...].astype(jnp.bfloat16)
        comb[1, :, j * HD : (j + 1) * HD] = acc_v[...].astype(jnp.bfloat16)
        for s in range(1, n):
            e_copy(s, j).start()
        e_local(j).start()
        if j == 0:
            pass_on(1)
    for s in range(2, n):
        pass_on(s)
        pass_over(s - 1)
    pass_over(n - 1)
    own.wait()
    for j in range(local_heads):
        e_local(j).wait()
    for s in range(1, n):
        share(s, sibling, sb_s, sb_r, sibling).wait_recv()
        share(s, far, fw_s, fw_r, sibling).wait_recv()
        z_copy(s).wait_send()
        share(s, t, ac_s, ac_r, across).wait_send()
        share(s, t, sb_s, sb_r, sibling).wait_send()
        share(s, across, fw_s, fw_r, sibling).wait_send()
        for j in range(local_heads):
            e_copy(s, j).wait()


def attention(n, normed, queries, out_grad, keys, values):
    tokens, width = queries.shape
    kv = keys.shape[1]
    depth = normed.shape[1] // n
    dma = pltpu.SemaphoreType.DMA
    hbm = pl.BlockSpec(memory_space=pl.ANY)
    vmem = pl.BlockSpec(memory_space=pltpu.VMEM)
    return pl.pallas_call(
        functools.partial(attention_kernel, n),
        out_shape=[
            jax.ShapeDtypeStruct((tokens, width), jnp.bfloat16),
            jax.ShapeDtypeStruct((n, tokens, depth), jnp.bfloat16),
            jax.ShapeDtypeStruct((2, n, tokens, kv), jnp.bfloat16),
        ],
        in_specs=[hbm] + [vmem] * 4,
        out_specs=[vmem, hbm, hbm],
        scratch_shapes=[
            pltpu.VMEM((2, tokens, kv), jnp.bfloat16),
            pltpu.VMEM((tokens, HD), jnp.float32),
            pltpu.VMEM((tokens, HD), jnp.float32),
            dma((1 + kv // HD,)),
        ]
        + [dma((n,))] * 8
        + [dma((n, kv // HD))] * 2,
        compiler_params=pltpu.CompilerParams(
            collective_id=1, has_side_effects=True, vmem_limit_bytes=44 * 2**20
        ),
        name="attention_and_exchange",
    )(normed, queries, out_grad, keys, values)


def shards(n, hidden_in, norm_gain, queries, key_weight, value_weight, out_grad):
    depth, kv_width = key_weight.shape
    whole, gains, all_key, all_value = gather_all(n, hidden_in[0], norm_gain, key_weight, value_weight)
    wide = whole.astype(jnp.float32)
    power = jnp.mean(wide * wide, axis=-1, keepdims=True)
    normed = (wide * lax.rsqrt(power + 1e-05) * gains.reshape(-1).astype(jnp.float32)).astype(jnp.bfloat16)
    keys = jnp.dot(normed, all_key.reshape(-1, kv_width), preferred_element_type=jnp.float32)
    values = jnp.dot(normed, all_value.reshape(-1, kv_width), preferred_element_type=jnp.float32)
    attended, columns, every = attention(
        n, normed, queries[0], out_grad[0], keys.astype(jnp.bfloat16), values.astype(jnp.bfloat16)
    )
    columns = columns.reshape(-1, depth)
    swap = [(0, 1), (1, 0)]
    grads = []
    for i in range(2):
        term = lax.dot_general(
            columns, every[i].reshape(-1, kv_width), (((0,), (0,)), ((), ())),
            preferred_element_type=jnp.float32,
        )
        grads.append(term + lax.ppermute(term, "dp", swap))
    return (attended[None], grads[0], grads[1])


def solution(mesh):
    placed = (
        P(("pipe", "dp"), None, "tensor"),
        P("tensor"),
        P(("pipe", "dp"), None, "tensor"),
        P("pipe", "tensor"),
        P("pipe", "tensor"),
        P(("pipe", "dp"), None, "tensor"),
    )
    return jax.shard_map(
        functools.partial(shards, mesh.shape["pipe"]),
        mesh=mesh,
        in_specs=placed,
        out_specs=(P(("pipe", "dp"), None, "tensor"), P("pipe", "tensor"), P("pipe", "tensor")),
        check_vma=False,
    )
```

```python
import functools
import jax
import jax.numpy as jnp
from jax import lax
from jax.experimental import pallas as pl
from jax.experimental.pallas import tpu as pltpu
from jax.sharding import PartitionSpec as P

HD = 128
GROUP = 8
MESH = pl.DeviceIdType.MESH


def gather_kernel(
    n, wc, g_in, k_in, v_in, g_out, k_out, v_out,
    loc_sem, g_s, g_r, zu_s, zd_s, z_r, y_s, y_r,
):
    p = lax.axis_index("pipe")
    d = lax.axis_index("dp")
    t = lax.axis_index("tensor")
    a, c = t // 2, t % 2
    across, sibling = (1 - a) * 2 + c, a * 2 + (1 - c)
    far = (1 - a) * 2 + (1 - c)
    depth = k_in.shape[0]
    half = depth // 2
    piece = half // wc

    barrier = pltpu.get_barrier_semaphore()
    for peer in (across, sibling, far):
        pl.semaphore_signal(barrier, inc=1, device_id=(p, d, peer), device_id_type=MESH)
    pl.semaphore_signal(barrier, inc=1, device_id=(p, 1 - d, t), device_id_type=MESH)

    for peer in (lax.rem(p + 1, n), lax.rem(p + n - 1, n)):
        pl.semaphore_signal(barrier, inc=1, device_id=(peer, d, t), device_id_type=MESH)
    pl.semaphore_wait(barrier, 6)

    def remote(src, dst, ssem, rsem, dev):
        return pltpu.make_async_remote_copy(
            src_ref=src, dst_ref=dst, send_sem=ssem, recv_sem=rsem, device_id=dev, device_id_type=MESH
        )

    def wpart(ref, b, k, hd):
        return ref.at[b, pl.ds(hd * half + (k % wc) * piece, piece)]

    def wout(k):
        return k_out if k < wc else v_out

    def wsrc(k):
        return (k_in if k < wc else v_in).at[pl.ds(d * half + (k % wc) * piece, piece)]

    def z_copy(src, b, k, up):
        dev = (p + 1, d, t) if up else (p - 1, d, t)
        sem = zu_s if up else zd_s
        return remote(src, wpart(wout(k), b, k, d), sem.at[b, k], z_r.at[b, k], dev)

    def y_copy(b, k, hd):
        part = wpart(wout(k), b, k, hd)
        return remote(part, part, y_s.at[b, k], y_r.at[b, k], (p, 1 - d, t))

    for k in range(2 * wc):

        @pl.when(p < n - 1)
        def _(k=k):
            z_copy(wsrc(k), p, k, True).start()

        @pl.when(p > 0)
        def _(k=k):
            z_copy(wsrc(k), p, k, False).start()

    gains = [
        remote(g_in, g_out.at[t], g_s.at[i], g_r.at[i], (p, d, peer))
        for i, peer in enumerate((across, sibling, far))
    ]
    for copy in gains:
        copy.start()
    local = [
        pltpu.make_async_copy(g_in, g_out.at[t], loc_sem.at[0]),
        pltpu.make_async_copy(k_in, k_out.at[p], loc_sem.at[1]),
        pltpu.make_async_copy(v_in, v_out.at[p], loc_sem.at[2]),
    ]
    for copy in local:
        copy.start()

    for s in range(1, n):
        for k in range(2 * wc):

            @pl.when(p - s >= 0)
            def _(s=s, k=k):
                b = p - s
                z_copy(wsrc(k), b, k, True).wait_recv()

                @pl.when(p < n - 1)
                def _():
                    z_copy(wpart(wout(k), b, k, d), b, k, True).start()

                y_copy(b, k, d).start()

            @pl.when(p + s < n)
            def _(s=s, k=k):
                b = p + s
                z_copy(wsrc(k), b, k, False).wait_recv()

                @pl.when(p > 0)
                def _():
                    z_copy(wpart(wout(k), b, k, d), b, k, False).start()

                y_copy(b, k, d).start()

    for s in range(1, n):
        for k in range(2 * wc):
            for up in (True, False):
                b = p - s if up else p + s

                @pl.when((b >= 0) & (b < n))
                def _(b=b, k=k):
                    y_copy(b, k, 1 - d).wait_recv()
                    y_copy(b, k, d).wait_send()

    for s in range(n):
        for k in range(2 * wc):

            @pl.when((p - s >= 0) & (p < n - 1))
            def _(s=s, k=k):
                z_copy(wsrc(k), p - s, k, True).wait_send()

            @pl.when((p + s < n) & (p > 0))
            def _(s=s, k=k):
                z_copy(wsrc(k), p + s, k, False).wait_send()

    for i, peer in enumerate((across, sibling, far)):
        remote(g_in, g_out.at[peer], g_s.at[i], g_r.at[i], (p, d, peer)).wait_recv()
    for copy in gains:
        copy.wait_send()
    for copy in local:
        copy.wait()


def gather_weights(n, gain, key_weight, value_weight):
    depth, kv = key_weight.shape
    gain = gain.reshape(-1, 128)
    wc = 2 if n <= 8 else 1
    dma = pltpu.SemaphoreType.DMA
    any_spec = pl.BlockSpec(memory_space=pl.ANY)
    return pl.pallas_call(
        functools.partial(gather_kernel, n, wc),
        out_shape=[
            jax.ShapeDtypeStruct((4,) + gain.shape, gain.dtype),
            jax.ShapeDtypeStruct((n, depth, kv), key_weight.dtype),
            jax.ShapeDtypeStruct((n, depth, kv), value_weight.dtype),
        ],
        in_specs=[any_spec] * 3,
        out_specs=[any_spec] * 3,
        scratch_shapes=[
            dma((3,)),
            dma((3,)), dma((3,)),
            dma((n, 2 * wc)), dma((n, 2 * wc)), dma((n, 2 * wc)), dma((n, 2 * wc)), dma((n, 2 * wc)),
        ],
        compiler_params=pltpu.CompilerParams(collective_id=0, has_side_effects=True),
        name="gather_weights",
        cost_estimate=pl.CostEstimate(flops=8 * 10**10, bytes_accessed=2 * 10**8, transcendentals=0),
    )(gain, key_weight, value_weight)


def attention_kernel(
    n, normed, q_ref, g_ref, k_ref, v_ref, att_ref, x_out, e_out, comb, acc_k, acc_v,
    loc_sem, z_s, z_r, ac_s, ac_r, sb_s, sb_r, fw_s, fw_r, e_s, e_r,
):
    p = lax.axis_index("pipe")
    d = lax.axis_index("dp")
    t = lax.axis_index("tensor")
    a, c = t // 2, t % 2
    across, sibling = (1 - a) * 2 + c, a * 2 + (1 - c)
    far = (1 - a) * 2 + (1 - c)
    tokens = q_ref.shape[0]
    depth = x_out.shape[2]
    quarter = tokens // 4
    scale = 1.0 / HD**0.5
    local_heads = k_ref.shape[1] // HD
    group = q_ref.shape[1] // HD // local_heads

    barrier = pltpu.get_barrier_semaphore()
    for s in range(1, n):
        pl.semaphore_signal(barrier, inc=1, device_id=(lax.rem(p + s, n), d, t), device_id_type=MESH)
    for peer in (across, sibling):
        pl.semaphore_signal(barrier, inc=1, device_id=(p, d, peer), device_id_type=MESH)
    pl.semaphore_wait(barrier, n + 1)

    def remote(src, dst, ssem, rsem, dev):
        return pltpu.make_async_remote_copy(
            src_ref=src, dst_ref=dst, send_sem=ssem, recv_sem=rsem, device_id=dev, device_id_type=MESH
        )

    def rows(i):
        return pl.ds(pl.multiple_of(i * quarter, quarter), quarter)

    def cols(i):
        return pl.ds(pl.multiple_of(i * depth, depth), depth)

    def z_copy(s):
        dest = lax.rem(p + s, n)
        return remote(
            normed.at[rows(t), cols(dest)], x_out.at[s, rows(t)], z_s.at[s], z_r.at[s], (dest, d, t)
        )

    def share(s, part, ssem, rsem, peer):
        ref = x_out.at[s, rows(part)]
        return remote(ref, ref, ssem.at[s], rsem.at[s], (p, d, peer))

    def e_copy(s, j):
        dest = lax.rem(p + s, n)
        width = pl.ds(j * HD, HD)
        return remote(
            comb.at[:, :, width], e_out.at[:, s, :, width], e_s.at[s, j], e_r.at[s, j], (dest, d, t)
        )

    def e_local(j):
        width = pl.ds(j * HD, HD)
        return pltpu.make_async_copy(comb.at[:, :, width], e_out.at[:, 0, :, width], loc_sem.at[1 + j])

    def pass_on(s):
        z_copy(s).wait_recv()
        share(s, t, ac_s, ac_r, across).start()
        share(s, t, sb_s, sb_r, sibling).start()

    def pass_over(s):
        share(s, across, ac_s, ac_r, across).wait_recv()
        share(s, across, fw_s, fw_r, sibling).start()

    for s in range(1, n):
        z_copy(s).start()
    own = pltpu.make_async_copy(normed.at[:, cols(p)], x_out.at[0], loc_sem.at[0])
    own.start()

    blocks = 2
    size = tokens // blocks
    nt = (((1,), (1,)), ((), ()))
    tn = (((0,), (0,)), ((), ()))
    f32 = jnp.float32
    for j in range(local_heads):
        acc_k[...] = jnp.zeros_like(acc_k)
        acc_v[...] = jnp.zeros_like(acc_v)

        def head(i, carry, j=j):
            at = pl.ds(pl.multiple_of((j * group + i) * HD, HD), HD)
            for b in range(blocks):
                low, high = b * size, (b + 1) * size
                q = q_ref[low:high, at]
                g = g_ref[low:high, at]
                k = k_ref[:high, j * HD : (j + 1) * HD]
                v = v_ref[:high, j * HD : (j + 1) * HD]
                scores = lax.dot_general(q, k, nt, preferred_element_type=f32) * scale
                qpos = low + lax.broadcasted_iota(jnp.int32, scores.shape, 0)
                kpos = lax.broadcasted_iota(jnp.int32, scores.shape, 1)
                scores = jnp.where(qpos >= kpos, scores, -1e30)
                top = jnp.max(scores, axis=-1, keepdims=True)
                e = jnp.exp(scores - top)
                probs = e * (1.0 / jnp.sum(e, axis=-1, keepdims=True))
                low_probs = probs.astype(jnp.bfloat16)
                att = jnp.dot(low_probs, v, preferred_element_type=f32)
                att_ref[low:high, at] = att.astype(jnp.bfloat16)
                dprobs = lax.dot_general(g, v, nt, preferred_element_type=f32)
                inner = jnp.sum(dprobs * probs, axis=-1, keepdims=True)
                dscores = (probs * (dprobs - inner) * scale).astype(jnp.bfloat16)
                acc_v[:high] += lax.dot_general(low_probs, g, tn, preferred_element_type=f32)
                acc_k[:high] += lax.dot_general(dscores, q, tn, preferred_element_type=f32)
            return carry

        lax.fori_loop(0, group, head, 0)
        comb[0, :, j * HD : (j + 1) * HD] = acc_k[...].astype(jnp.bfloat16)
        comb[1, :, j * HD : (j + 1) * HD] = acc_v[...].astype(jnp.bfloat16)
        for s in range(1, n):
            e_copy(s, j).start()
        e_local(j).start()
        if j == 0:
            pass_on(1)
    for s in range(2, n):
        pass_on(s)
        pass_over(s - 1)
    pass_over(n - 1)
    own.wait()
    for j in range(local_heads):
        e_local(j).wait()
    for s in range(1, n):
        share(s, sibling, sb_s, sb_r, sibling).wait_recv()
        share(s, far, fw_s, fw_r, sibling).wait_recv()
        z_copy(s).wait_send()
        share(s, t, ac_s, ac_r, across).wait_send()
        share(s, t, sb_s, sb_r, sibling).wait_send()
        share(s, across, fw_s, fw_r, sibling).wait_send()
        for j in range(local_heads):
            e_copy(s, j).wait()


def attention(n, normed, queries, out_grad, keys, values):
    tokens, width = queries.shape
    kv = keys.shape[1]
    depth = normed.shape[1] // n
    dma = pltpu.SemaphoreType.DMA
    hbm = pl.BlockSpec(memory_space=pl.ANY)
    vmem = pl.BlockSpec(memory_space=pltpu.VMEM)
    return pl.pallas_call(
        functools.partial(attention_kernel, n),
        out_shape=[
            jax.ShapeDtypeStruct((tokens, width), jnp.bfloat16),
            jax.ShapeDtypeStruct((n, tokens, depth), jnp.bfloat16),
            jax.ShapeDtypeStruct((2, n, tokens, kv), jnp.bfloat16),
        ],
        in_specs=[hbm] + [vmem] * 4,
        out_specs=[vmem, hbm, hbm],
        scratch_shapes=[
            pltpu.VMEM((2, tokens, kv), jnp.bfloat16),
            pltpu.VMEM((tokens, HD), jnp.float32),
            pltpu.VMEM((tokens, HD), jnp.float32),
            dma((1 + kv // HD,)),
        ]
        + [dma((n,))] * 8
        + [dma((n, kv // HD))] * 2,
        compiler_params=pltpu.CompilerParams(
            collective_id=1, has_side_effects=True, vmem_limit_bytes=44 * 2**20
        ),
        name="attention_and_exchange",
    )(normed, queries, out_grad, keys, values)


def shards(n, hidden_in, norm_gain, queries, key_weight, value_weight, out_grad):
    depth, kv_width = key_weight.shape
    whole = lax.all_gather(hidden_in[0], "tensor", axis=1, tiled=True)
    gains, all_key, all_value = gather_weights(n, norm_gain, key_weight, value_weight)
    wide = whole.astype(jnp.float32)
    power = jnp.mean(wide * wide, axis=-1, keepdims=True)
    normed = (wide * lax.rsqrt(power + 1e-05) * gains.reshape(-1).astype(jnp.float32)).astype(jnp.bfloat16)
    keys = jnp.dot(normed, all_key.reshape(-1, kv_width), preferred_element_type=jnp.float32)
    values = jnp.dot(normed, all_value.reshape(-1, kv_width), preferred_element_type=jnp.float32)
    attended, columns, every = attention(
        n, normed, queries[0], out_grad[0], keys.astype(jnp.bfloat16), values.astype(jnp.bfloat16)
    )
    columns = columns.reshape(-1, depth)
    swap = [(0, 1), (1, 0)]
    grads = []
    for i in range(2):
        term = lax.dot_general(
            columns, every[i].reshape(-1, kv_width), (((0,), (0,)), ((), ())),
            preferred_element_type=jnp.float32,
        )
        term = lax.reduce_precision(term, 8, 7)
        other = lax.ppermute(term.astype(jnp.bfloat16), "dp", swap)
        grads.append(term + other.astype(jnp.float32))
    return (attended[None], grads[0], grads[1])


def solution(mesh):
    placed = (
        P(("pipe", "dp"), None, "tensor"),
        P("tensor"),
        P(("pipe", "dp"), None, "tensor"),
        P("pipe", "tensor"),
        P("pipe", "tensor"),
        P(("pipe", "dp"), None, "tensor"),
    )
    return jax.shard_map(
        functools.partial(shards, mesh.shape["pipe"]),
        mesh=mesh,
        in_specs=placed,
        out_specs=(P(("pipe", "dp"), None, "tensor"), P("pipe", "tensor"), P("pipe", "tensor")),
        check_vma=False,
    )
```
